512 devices in a mesh: layer: 2 (over core), latent: 32 (over z_hi, y, x), token: 8 (over z_lo).
Axes of the slice: x: 4, y: 4, z: 16 (z_hi: 2, z_lo: 8; z = z_hi * 8 + z_lo), core: 2. Of those that a mesh axis runs over, the one named last changes fastest.
Arguments:
- taps: bfloat16 [2, 1792, 3584], P('layer', 'token'), may hold values from -6 to 6
- token_ids: int32 [1792], P('token'), may hold values from 2 to 255999, as said below
- enc_weight: bfloat16 [2, 3584, 8192], P('layer', 'token', 'latent'), may hold values from -0.0625 to 0.0625
- enc_bias: float32 [8192], P('latent'), may hold values from -3 to 3
- dec_weight: bfloat16 [2, 3584, 8192], P('layer', 'token', 'latent'), as said below
- dec_bias: float32 [2, 3584], P('layer'), may hold values from -3 to 3
Outputs:
- enc_grad: bfloat16 [2, 3584, 8192], P('layer', 'token', 'latent')
- dec_grad: bfloat16 [2, 3584, 8192], P('layer', 'token', 'latent')
The draws below stay inside these ranges and needn't reach their ends.
Inputs may be any that keep to these rules, and one draw needn't show every extreme that they name: `token_ids`: id 2 marks the beginning of a document and stands at position 0; all other ids are 3 or more. `dec_weight`: entries of order 8192^-0.5.
All inputs are finite; a program needn't handle non-finite values.
Results may differ from the reference program's by a relative error of at most 0.014.
Values may be sent and summed in bfloat16 or wider, within the bound.
A program may use at most 64 MiB of HBM per device.

```python
import math
import jax
import jax.numpy as jnp
from jax import lax

D = 3584
VOCAB = 256000
TOK_DEV = 224
LATENTS = 8192
LAYERS = 2
TOKENS = 1792
N_TOKEN = 8


def draw_token_ids(key, part):
    folded = jax.random.fold_in(key, 11)
    word_key, begin_key = jax.random.split(folded)
    vocab_ids = jax.random.randint(word_key, (TOKENS,), 3, VOCAB, dtype=jnp.int32)
    starts = jax.random.randint(begin_key, (TOKENS,), 0, 16, dtype=jnp.int32) == 0
    position = jnp.arange(TOKENS, dtype=jnp.int32)
    starts = jnp.logical_or(starts, position == 0)
    return jnp.where(starts, 2, vocab_ids).astype(jnp.int32)


def draw_dec_weight(key, part):
    folded = jax.random.fold_in(key, 23)
    entry_key, row_key, col_key = jax.random.split(folded, 3)
    entries = jax.random.truncated_normal(entry_key, -6.0, 6.0, (LAYERS, D, LATENTS), jnp.float32)
    lower = 0.32
    upper = 3.2
    row_scale = jnp.exp(jax.random.uniform(row_key, (LAYERS, D, 1), jnp.float32, math.log(lower), math.log(upper)))
    col_scale = jnp.exp(jax.random.uniform(col_key, (LAYERS, 1, LATENTS), jnp.float32, math.log(lower), math.log(upper)))
    return (entries * row_scale * col_scale / math.sqrt(5.0 * LATENTS)).astype(jnp.bfloat16)


def block_levels(key, shape, pieces, smallest, largest):
    level, own = 1.0, jax.random.fold_in(key, 6)
    for dim, blocks in pieces:
        steps = jnp.exp(jax.random.uniform(jax.random.fold_in(own, dim), (blocks,), jnp.float32, smallest / len(pieces), largest / len(pieces)))
        level = level * jnp.repeat(steps, shape[dim] // blocks).reshape([-1 if axis == dim else 1 for axis in range(len(shape))])
    return level


def normal_values(own_key, dims, deviation, reach, cuts=(), held_as=jnp.bfloat16):
    result = jax.random.normal(own_key, dims, jnp.float32) * deviation
    if len(cuts) > 0:
        result = block_levels(own_key, dims, cuts, -0.22, 0.18) * result
    return jnp.clip(result, min=-reach, max=reach).astype(held_as)


def setup_inputs(seed: int = 0) -> dict:
    keys = jax.random.split(jax.random.key(seed), 7)
    return {
        "taps": normal_values(keys[0], (LAYERS, TOKENS, D), 1.0, 6.0, ((0, 2), (1, 8))),
        "token_ids": draw_token_ids(jax.random.fold_in(keys[6], 71), 0),
        "enc_weight": normal_values(keys[2], (LAYERS, D, LATENTS), (LAYERS * D) ** -0.5, 0.0625, ((0, 2), (1, 8), (2, 32))),
        "enc_bias": normal_values(keys[3], (LATENTS,), 0.5, 3.0, ((0, 32),), jnp.float32),
        "dec_weight": draw_dec_weight(jax.random.fold_in(keys[6], 71), 0),
        "dec_bias": normal_values(keys[5], (LAYERS, D), 0.5, 3.0, ((0, 2),), jnp.float32),
    }


KNEE_WIDTH = 0.5
SPARSITY = 0.5
BEGIN_TOKEN = 2

def smooth_relu(preact):
    positive = jnp.maximum(preact, 0.0)
    return jnp.where(positive < KNEE_WIDTH, positive * positive / (2.0 * KNEE_WIDTH), positive - 0.5 * KNEE_WIDTH)

def relu_slope(preact):
    return jnp.clip(preact / KNEE_WIDTH, 0.0, 1.0)

def reference(taps, token_ids, enc_weight, enc_bias, dec_weight, dec_bias):
    loss_scale = 1.0 / math.sqrt(TOKENS)
    keep_mask = (token_ids != BEGIN_TOKEN).astype(jnp.float32)
    preact = jnp.zeros((TOKENS, LATENTS), jnp.float32) + enc_bias[None, :]
    for layer_index in range(LAYERS):
        preact = preact + jnp.dot(taps[layer_index], enc_weight[layer_index], preferred_element_type=jnp.float32)
    features = smooth_relu(preact).astype(jnp.bfloat16)
    colnorm = jnp.sqrt(lax.optimization_barrier(jnp.sum(jnp.square(dec_weight.astype(jnp.float32)), axis=1)) + 1e-06)
    feat_grads = loss_scale * SPARSITY * keep_mask[:, None] * lax.optimization_barrier(jnp.sum(colnorm, axis=0))[None, :]
    residues = []
    for layer_index in range(LAYERS):
        rebuilt = lax.dot_general(features, dec_weight[layer_index], (((1,), (1,)), ((), ())), preferred_element_type=jnp.float32)
        rebuilt = rebuilt + dec_bias[layer_index][None, :]
        residue = (loss_scale * keep_mask[:, None] * (rebuilt - taps[layer_index].astype(jnp.float32))).astype(jnp.bfloat16)
        residues.append(residue)
        feat_grads = feat_grads + jnp.dot(residue, dec_weight[layer_index], preferred_element_type=jnp.float32)
    pre_grads = (feat_grads * relu_slope(preact)).astype(jnp.bfloat16)
    enc_grads = []
    dec_grads = []
    for layer_index in range(LAYERS):
        enc_total = jnp.zeros((D, LATENTS), jnp.float32)
        dec_total = jnp.zeros((D, LATENTS), jnp.float32)
        normed = dec_weight[layer_index].astype(jnp.float32) / colnorm[layer_index][None, :]
        for block_index in range(N_TOKEN):
            first_row = block_index * TOK_DEV
            tap_block = taps[layer_index, first_row:first_row + TOK_DEV]
            grad_block = pre_grads[first_row:first_row + TOK_DEV]
            feat_block = features[first_row:first_row + TOK_DEV]
            residue_block = residues[layer_index][first_row:first_row + TOK_DEV]
            mask_block = keep_mask[first_row:first_row + TOK_DEV]
            enc_term = lax.dot_general(tap_block, grad_block, (((0,), (0,)), ((), ())), preferred_element_type=jnp.float32)
            enc_total = enc_total + lax.optimization_barrier(enc_term.astype(jnp.bfloat16)).astype(jnp.float32)
            activity = lax.optimization_barrier(jnp.sum(mask_block[:, None] * feat_block.astype(jnp.float32), axis=0))
            dec_term = lax.dot_general(residue_block, feat_block, (((0,), (0,)), ((), ())), preferred_element_type=jnp.float32)
            dec_term = dec_term + loss_scale * SPARSITY * activity[None, :] * normed
            dec_total = dec_total + lax.optimization_barrier(dec_term.astype(jnp.bfloat16)).astype(jnp.float32)
        enc_grads.append(enc_total.astype(jnp.bfloat16))
        dec_grads.append(dec_total.astype(jnp.bfloat16))
    return (jnp.stack(enc_grads), jnp.stack(dec_grads))
```

```python
import functools
import math

import jax
import jax.numpy as jnp
from jax import lax
from jax.experimental import pallas as pl
from jax.experimental.pallas import tpu as pltpu
from jax.sharding import PartitionSpec as P

KNEE_WIDTH = 0.5
SPARSITY = 0.5
BEGIN_TOKEN = 2
MESH = pl.DeviceIdType.MESH
F32 = jnp.float32
BF16 = jnp.bfloat16

CHUNKS = 2
ROWS = 112
TILES = 7
PAIR = 896
SHARES = 14


def smooth_relu(preact):
    positive = jnp.maximum(preact, 0.0)
    return jnp.where(
        positive < KNEE_WIDTH, positive * positive / (2.0 * KNEE_WIDTH), positive - 0.5 * KNEE_WIDTH
    )


def relu_slope(preact):
    return jnp.clip(preact / KNEE_WIDTH, 0.0, 1.0)


def kernel(loss_scale, taps, ids, we, eb, wd, db, enc_out, dec_out,
           x_t, w_e, w_d, mask, keep, nsq, cnorm, cnorm_o,
           pre_f, pre_x, pre_s, pre_r, pre_own, feat, reb, reb_r, zs, zb, zr, res,
           g_f, g_x, g_s, g_r, g_own, pg, dwd, dwd_s, dwd_r, dwe, dwe_s, dwe_r,
           loc, xz_s, xz_r, xy_s, xy_r, mk_s, mk_r, ns_s, ns_r, one_s, one_r,
           co_s, co_r, zg_s, zg_r, rr_s, rr_r, zh_s, zh_r, rs_s, rs_r):
    layer = lax.axis_index("layer")
    n = lax.axis_index("latent")
    m = lax.axis_index("token")
    h = n // 16
    y = (n // 4) % 4
    x = n % 4
    s = n % 16
    p = m // 2
    r = m % 2

    other_core = (1 - layer, n, m)
    twin = (layer, n, 2 * p + 1 - r)
    far = (layer, (1 - h) * 16 + s, m)

    def zpeer(k):
        return (layer, n, 2 * ((p + k) % 4) + r)

    def xy_to(k):
        return ((y + k // 4) % 4) * 4 + (x + k % 4) % 4

    def xy_from(k):
        return ((y + 4 - k // 4) % 4) * 4 + (x + 4 - k % 4) % 4

    def xypeer(k):
        return (layer, h * 16 + xy_to(k), m)

    def half(i):
        return pl.ds(pl.multiple_of(i * 128, 128), 128)

    mine, theirs = half(layer), half(1 - layer)
    cols = pl.ds(pl.multiple_of(p * PAIR, 128), PAIR)

    def share(i):
        return pl.ds((i // TILES) * 2, 2), pl.ds(pl.multiple_of((i % TILES) * 16, 16), 16)

    def remote(src, dst, send, recv, dev):
        return pltpu.make_async_remote_copy(
            src_ref=src, dst_ref=dst, send_sem=send, recv_sem=recv, device_id=dev, device_id_type=MESH
        )

    local = [
        pltpu.make_async_copy(taps.at[pl.ds(ROWS * c, ROWS), cols], x_t.at[c, 0], loc.at[c])
        for c in range(CHUNKS)
    ]
    local.append(pltpu.make_async_copy(we, w_e.at[r], loc.at[CHUNKS]))
    local.append(pltpu.make_async_copy(wd, w_d.at[r], loc.at[CHUNKS + 1]))
    for cp in local:
        cp.start()

    barrier = pltpu.get_barrier_semaphore()
    partners = [other_core, twin, far] + [zpeer(k) for k in (1, 2, 3)] + [xypeer(k) for k in range(1, 16)]
    for dev in partners:
        pl.semaphore_signal(barrier, inc=1, device_id=dev, device_id_type=MESH)
    keep_row = (ids[...] != BEGIN_TOKEN).astype(F32)
    mask[0] = jnp.broadcast_to(keep_row, mask.shape[1:]).astype(BF16)
    pl.semaphore_wait(barrier, len(partners))

    sends = []

    def go(cp):
        cp.start()
        sends.append(cp)
        return cp

    owns = s < SHARES

    s_in = lax.min(s, SHARES - 1)
    s_chunk, s_row = s_in // TILES, pl.ds(pl.multiple_of((s_in % TILES) * 16, 16), 16)
    s_src = pl.ds(pl.multiple_of(s_in * 16, 16), 16)

    def xz(k):
        there = pl.ds(pl.multiple_of(((p + k) % 4) * PAIR, 128), PAIR)
        return remote(taps.at[s_src, there], x_t.at[s_chunk, 4 - k, s_row], xz_s.at[k - 1], xz_r.at[3 - k], zpeer(k))

    def xz_here(k):
        return remote(taps.at[s_src, cols], x_t.at[s_chunk, 4 - k, s_row], xz_s.at[k - 1], xz_r.at[3 - k], zpeer(k))

    @pl.when(owns)
    def _():
        for k in (1, 2, 3):
            xz(k).start()

    we_cp = go(remote(we, w_e.at[r], one_s.at[0], one_r.at[0], twin))
    wd_cp = go(remote(wd, w_d.at[r], one_s.at[1], one_r.at[1], twin))
    mask_cp = [go(remote(mask.at[0], mask.at[4 - k], mk_s.at[k - 1], mk_r.at[3 - k], zpeer(k))) for k in (1, 2, 3)]

    def xy(k, row_chunk, row):
        part = x_t.at[row_chunk, pl.ds(1, 3), row]
        return remote(part, part, xy_s.at[k - 1], xy_r.at[k - 1], xypeer(k))

    @pl.when(owns)
    def _():
        for k in (1, 2, 3):
            xz_here(k).wait_recv()
        for k in range(1, 16):
            xy(k, s_chunk, s_row).start()

    for cp in local:
        cp.wait()
    wd_cp.wait_recv()
    w_sq = jnp.square(w_d[...].astype(F32)).reshape(PAIR, 256)
    nsq[0] = jnp.broadcast_to(jnp.sum(w_sq, axis=0, keepdims=True), (8, 256))
    ns_cp = [go(remote(nsq.at[0], nsq.at[4 - k], ns_s.at[k - 1], ns_r.at[3 - k], zpeer(k))) for k in (1, 2, 3)]
    for cp in mask_cp:
        cp.wait_recv()
    unit = jnp.full((16, 128), 1.0 / 16.0, BF16)
    for q in range(4):
        column = lax.dot_general(mask[q], unit, (((0,), (0,)), ((), ())), preferred_element_type=F32)
        for c in range(CHUNKS):
            keep[c, q] = column[c * ROWS:(c + 1) * ROWS]
    for cp in ns_cp:
        cp.wait_recv()
    cnorm[...] = jnp.sqrt(nsq[0] + nsq[1] + nsq[2] + nsq[3] + 1e-06)
    cn_cp = go(remote(cnorm, cnorm_o, one_s.at[2], one_r.at[2], other_core))
    we_cp.wait_recv()

    for k in range(1, 16):
        source = xy_from(k)

        @pl.when(source < SHARES)
        def _():
            there = lax.min(source, SHARES - 1)
            row = pl.ds(pl.multiple_of((there % TILES) * 16, 16), 16)
            xy(k, there // TILES, row).wait_recv()

    def z_group(sem, src, dst, c):
        return [
            go(remote(src(k), dst(4 - k), zg_s.at[sem, c, k - 1], zg_r.at[sem, c, 3 - k], zpeer(k)))
            for k in (1, 2, 3)
        ]

    enc = w_e[...].reshape(PAIR, 256)
    dec = w_d[...].reshape(PAIR, 256)

    def cross(c, sem, full, got):
        return go(remote(full.at[c, :, :, theirs], got.at[c], co_s.at[sem, c], co_r.at[sem, c], other_core))

    step = {}
    for c in range(CHUNKS):
        part = jnp.dot(x_t[c].reshape(4 * ROWS, PAIR), enc, preferred_element_type=F32)
        pre_f[c] = part.reshape(4, ROWS, 256)
        step["pc", c] = cross(c, 0, pre_f, pre_x)
    for c in range(CHUNKS):
        step["pc", c].wait_recv()
        pre_own[c] = pre_f[c, 0, :, mine] + pre_x[c, 0]
        for q in (1, 2, 3):
            pre_s[c, q - 1] = (pre_f[c, q, :, mine] + pre_x[c, q]).astype(BF16)
        step["pz", c] = z_group(0, lambda k: pre_s.at[c, k - 1], lambda q: pre_r.at[c, q - 1], c)
    for c in range(CHUNKS):
        for cp in step["pz", c]:
            cp.wait_recv()
        preact = pre_own[c] + eb[:, mine]
        for q in range(3):
            preact = preact + pre_r[c, q].astype(F32)
        pre_own[c] = preact
        feat[c, 0, :, mine] = smooth_relu(preact).astype(BF16)
        step["fz", c] = z_group(1, lambda k: feat.at[c, 0, :, mine], lambda q: feat.at[c, q, :, mine], c)
    for c in range(CHUNKS):
        for cp in step["fz", c]:
            cp.wait_recv()
        block = feat.at[c, :, :, mine]
        step["fc", c] = go(remote(block, block, co_s.at[1, c], co_r.at[1, c], other_core))

    def rr(c, k):
        blocks, row = share(lax.min(xy_to(k), SHARES - 1))
        return remote(reb.at[c, blocks, row], reb_r.at[c, k - 1], rr_s.at[c, k - 1], rr_r.at[c, k - 1], xypeer(k))

    blocks, row = share(s_in)

    def rs(c, k, blocks, row):
        part = res.at[c, blocks, row]
        return remote(part, part, rs_s.at[c, k - 1], rs_r.at[c, k - 1], xypeer(k))

    def zh(c):
        return remote(zb.at[c], zr.at[c], zh_s.at[c], zh_r.at[c], far)

    for c in range(CHUNKS):
        step["fc", c].wait_recv()
        part = lax.dot_general(
            feat[c].reshape(4 * ROWS, 256), dec, (((1,), (1,)), ((), ())), preferred_element_type=F32
        )
        reb[c] = part.astype(BF16).reshape(4, ROWS, PAIR)
        for k in range(1, 16):

            @pl.when(xy_to(k) < SHARES)
            def _():
                rr(c, k).start()

    for c in range(CHUNKS):

        @pl.when(owns)
        def _():
            total = reb[c, blocks, row].astype(F32)
            for k in range(1, 16):
                rr(c, k).wait_recv()
                total = total + reb_r[c, k - 1].astype(F32)
            zs[c] = total
            zb[c] = total.astype(BF16)
            zh(c).start()

    for c in range(CHUNKS):

        @pl.when(owns)
        def _():
            zh(c).wait_recv()
            rebuilt = zs[c] + zr[c].astype(F32) + db[:, cols].reshape(1, 1, PAIR)
            diff = rebuilt - x_t[c, blocks, row].astype(F32)
            weight = loss_scale * keep[c, blocks, row][:, :, :1]
            res[c, blocks, row] = (weight * diff).astype(BF16)
            for k in range(1, 16):
                rs(c, k, blocks, row).start()

    for c in range(CHUNKS):
        for k in range(1, 16):
            source = xy_from(k)

            @pl.when(source < SHARES)
            def _():
                rs(c, k, *share(lax.min(source, SHARES - 1))).wait_recv()

        part = jnp.dot(res[c].reshape(4 * ROWS, PAIR), dec, preferred_element_type=F32)
        g_f[c] = part.reshape(4, ROWS, 256)
        step["gc", c] = cross(c, 2, g_f, g_x)
    cn_cp.wait_recv()
    for c in range(CHUNKS):
        step["gc", c].wait_recv()
        g_own[c] = g_f[c, 0, :, mine] + g_x[c, 0]
        for q in (1, 2, 3):
            g_s[c, q - 1] = (g_f[c, q, :, mine] + g_x[c, q]).astype(BF16)
        step["gz", c] = z_group(2, lambda k: g_s.at[c, k - 1], lambda q: g_r.at[c, q - 1], c)
    norm_total = cnorm[0:1, mine] + cnorm_o[0:1, mine]
    for c in range(CHUNKS):
        for cp in step["gz", c]:
            cp.wait_recv()
        grads = g_own[c] + loss_scale * SPARSITY * keep[c, 0] * norm_total
        for q in range(3):
            grads = grads + g_r[c, q].astype(F32)
        pg[c, 0, :, mine] = (grads * relu_slope(pre_own[c])).astype(BF16)
        step["qz", c] = z_group(3, lambda k: pg.at[c, 0, :, mine], lambda q: pg.at[c, q, :, mine], c)

    activity = jnp.zeros((1, 256), F32)
    for c in range(CHUNKS):
        f = feat[c].reshape(4 * ROWS, 256)
        k_col = keep[c].reshape(4 * ROWS, 128)[:, :1]
        activity = activity + jnp.sum(k_col * f.astype(F32), axis=0, keepdims=True)
    penalty = loss_scale * SPARSITY * activity / cnorm[0:1, :]
    total = dec.astype(F32) * penalty
    for c in range(CHUNKS):
        total = total + lax.dot_general(
            res[c].reshape(4 * ROWS, PAIR), feat[c].reshape(4 * ROWS, 256), (((0,), (0,)), ((), ())),
            preferred_element_type=F32,
        )
    dwd[...] = total.reshape(2, PAIR // 2, 256)
    dwd_s[...] = dwd[1 - r].astype(BF16)
    dwd_cp = go(remote(dwd_s, dwd_r, one_s.at[3], one_r.at[3], twin))

    for c in range(CHUNKS):
        for cp in step["qz", c]:
            cp.wait_recv()
        block = pg.at[c, :, :, mine]
        step["qc", c] = go(remote(block, block, co_s.at[3, c], co_r.at[3, c], other_core))
    total = jnp.zeros((PAIR, 256), F32)
    for c in range(CHUNKS):
        step["qc", c].wait_recv()
        total = total + lax.dot_general(
            x_t[c].reshape(4 * ROWS, PAIR), pg[c].reshape(4 * ROWS, 256), (((0,), (0,)), ((), ())),
            preferred_element_type=F32,
        )
    dwe[...] = total.reshape(2, PAIR // 2, 256)
    dwe_s[...] = dwe[1 - r].astype(BF16)
    dwe_cp = go(remote(dwe_s, dwe_r, one_s.at[4], one_r.at[4], twin))
    dwd_cp.wait_recv()
    dec_out[...] = (dwd[r] + dwd_r[...].astype(F32)).astype(BF16)
    dwe_cp.wait_recv()
    enc_out[...] = (dwe[r] + dwe_r[...].astype(F32)).astype(BF16)

    for cp in sends:
        cp.wait_send()

    @pl.when(owns)
    def _():
        for k in (1, 2, 3):
            xz(k).wait_send()
        for k in range(1, 16):
            xy(k, s_chunk, s_row).wait_send()
        for c in range(CHUNKS):
            zh(c).wait_send()
            for k in range(1, 16):
                rs(c, k, blocks, row).wait_send()

    for c in range(CHUNKS):
        for k in range(1, 16):

            @pl.when(xy_to(k) < SHARES)
            def _():
                rr(c, k).wait_send()


def local(taps, token_ids, enc_weight, enc_bias, dec_weight, dec_bias):
    tokens_dev = taps.shape[1]
    loss_scale = 1.0 / math.sqrt(tokens_dev * lax.axis_size("token"))
    c = CHUNKS
    dma = pltpu.SemaphoreType.DMA
    vmem = pltpu.VMEM
    scratch = [
        vmem((c, 4, ROWS, PAIR), BF16),
        vmem((2, 448, 256), BF16), vmem((2, 448, 256), BF16),
        vmem((4, 16, 224), BF16), vmem((c, 4, ROWS, 128), F32),
        vmem((4, 8, 256), F32), vmem((8, 256), F32), vmem((8, 256), F32),
        vmem((c, 4, ROWS, 256), F32), vmem((c, 4, ROWS, 128), F32),
        vmem((c, 3, ROWS, 128), BF16), vmem((c, 3, ROWS, 128), BF16), vmem((c, ROWS, 128), F32),
        vmem((c, 4, ROWS, 256), BF16),
        vmem((c, 4, ROWS, PAIR), BF16), vmem((c, 15, 2, 16, PAIR), BF16),
        vmem((c, 2, 16, PAIR), F32), vmem((c, 2, 16, PAIR), BF16), vmem((c, 2, 16, PAIR), BF16),
        vmem((c, 4, ROWS, PAIR), BF16),
        vmem((c, 4, ROWS, 256), F32), vmem((c, 4, ROWS, 128), F32),
        vmem((c, 3, ROWS, 128), BF16), vmem((c, 3, ROWS, 128), BF16), vmem((c, ROWS, 128), F32),
        vmem((c, 4, ROWS, 256), BF16),
        vmem((2, 448, 256), F32), vmem((448, 256), BF16), vmem((448, 256), BF16),
        vmem((2, 448, 256), F32), vmem((448, 256), BF16), vmem((448, 256), BF16),
        dma((c + 2,)),
        dma((3,)), dma((3,)), dma((15,)), dma((15,)), dma((3,)), dma((3,)), dma((3,)), dma((3,)),
        dma((5,)), dma((5,)),
        dma((4, c)), dma((4, c)), dma((4, c, 3)), dma((4, c, 3)),
        dma((c, 15)), dma((c, 15)), dma((c,)), dma((c,)), dma((c, 15)), dma((c, 15)),
    ]
    any_spec = pl.BlockSpec(memory_space=pl.ANY)
    vmem_spec = pl.BlockSpec(memory_space=pltpu.VMEM)
    enc_grad, dec_grad = pl.pallas_call(
        functools.partial(kernel, loss_scale),
        out_shape=(jax.ShapeDtypeStruct((448, 256), BF16), jax.ShapeDtypeStruct((448, 256), BF16)),
        in_specs=[any_spec, vmem_spec, any_spec, vmem_spec, any_spec, vmem_spec],
        out_specs=(vmem_spec, vmem_spec),
        scratch_shapes=scratch,
        compiler_params=pltpu.CompilerParams(
            collective_id=0, has_side_effects=True, vmem_limit_bytes=40 * 1024 * 1024
        ),
        name="crosscoder",
    )(taps[0], token_ids[None, :], enc_weight[0], enc_bias[None, :], dec_weight[0], dec_bias)
    return enc_grad[None], dec_grad[None]


def solution(mesh):
    placed = (
        P("layer", "token", None),
        P("token"),
        P("layer", "token", "latent"),
        P("latent"),
        P("layer", "token", "latent"),
        P("layer", None),
    )
    return jax.shard_map(
        local,
        mesh=mesh,
        in_specs=placed,
        out_specs=(P("layer", "token", "latent"), P("layer", "token", "latent")),
        check_vma=False,
    )
```

```python
import functools
import math

import jax
import jax.numpy as jnp
from jax import lax
from jax.experimental import pallas as pl
from jax.experimental.pallas import tpu as pltpu
from jax.sharding import PartitionSpec as P

KNEE_WIDTH = 0.5
SPARSITY = 0.5
BEGIN_TOKEN = 2
MESH = pl.DeviceIdType.MESH
F32 = jnp.float32
BF16 = jnp.bfloat16

CHUNKS = 2
ROWS = 112
PADDED = 128
TILES = 7
PAIR = 896

CHAIN = (
    "taps_first", "taps_second", "pre_dot", "pre_sum", "pre_act", "feat_cross", "reb_dot", "reb_mid", "reb_sum",
    "residue", "residue_second", "grad_dot", "grad_sum", "dec_grad", "grad_pre", "grad_cross", "enc_grad",
)
LAG = 1
ORDER = [
    (stage, c) for _, c, stage in sorted((i + LAG * c, c, s) for i, s in enumerate(CHAIN) for c in range(CHUNKS))
]
ORDER.insert(ORDER.index(("pre_sum", CHUNKS - 1)) + 1, ("norms_first", 0))
ORDER.insert(ORDER.index(("reb_dot", 0)) + 1, ("norms_second", 0))


def smooth_relu(preact):
    positive = jnp.maximum(preact, 0.0)
    return jnp.where(
        positive < KNEE_WIDTH, positive * positive / (2.0 * KNEE_WIDTH), positive - 0.5 * KNEE_WIDTH
    )


def relu_slope(preact):
    return jnp.clip(preact / KNEE_WIDTH, 0.0, 1.0)


def kernel(loss_scale, taps, ids_in, we, eb, wd, db, enc_out, dec_out,
           ids, bias, dbias, x_t, w_e, w_d, mask, keep, nsq, cnorm, cnorm_o,
           pre_f, pre_x, pre_s, pre_r, pre_own, feat, reb, row_r, col_r, row_s, col_s, own_s, end_r,
           zs, zb, zr, res, g_f, g_x, g_s, g_r, g_own, pg, dwd, dwd_s, dwd_r, dwe, dwe_s, dwe_r,
           loc, xz_s, xz_r, xy_s, xy_r, mk_s, mk_r, ns_s, ns_r, one_s, one_r,
           co_s, co_r, zg_s, zg_r, rr_s, rr_r, zh_s, zh_r, rs_s, rs_r):
    layer = lax.axis_index("layer")
    n = lax.axis_index("latent")
    m = lax.axis_index("token")
    h = n // 16
    y = (n // 4) % 4
    x = n % 4
    p = m // 2
    r = m % 2

    other_core = (1 - layer, n, m)
    twin = (layer, n, 2 * p + 1 - r)
    far = (layer, (1 - h) * 16 + n % 16, m)

    def zpeer(k):
        return (layer, n, 2 * ((p + k) % 4) + r)

    def chip(yy, xx):
        return (layer, h * 16 + yy * 4 + xx, m)

    def half(i):
        return pl.ds(pl.multiple_of(i * 128, 128), 128)

    mine, theirs = half(layer), half(1 - layer)
    cols = pl.ds(pl.multiple_of(p * PAIR, 128), PAIR)
    real = pl.ds(0, ROWS)

    def has_tile(yy, xx):
        return jnp.logical_not(jnp.logical_and(yy % 2 == 1, xx == 3))

    owns = has_tile(y, x)

    def remote(src, dst, send, recv, dev):
        return pltpu.make_async_remote_copy(
            src_ref=src, dst_ref=dst, send_sem=send, recv_sem=recv, device_id=dev, device_id_type=MESH
        )

    local = []
    for c in range(CHUNKS):
        local.append(pltpu.make_async_copy(taps.at[pl.ds(TILES * c, 4), :, cols], x_t.at[c, 0, 0, 0], loc.at[2 * c]))
        local.append(
            pltpu.make_async_copy(
                taps.at[pl.ds(TILES * c + 4, 3), :, cols], x_t.at[c, 0, 0, 1, pl.ds(0, 3)], loc.at[2 * c + 1]
            )
        )
    ids_cp = pltpu.make_async_copy(ids_in, ids, loc.at[2 * CHUNKS])
    ids_cp.start()
    local.append(pltpu.make_async_copy(eb.at[:, mine], bias, loc.at[2 * CHUNKS + 1]))
    local.append(pltpu.make_async_copy(db.at[:, cols], dbias, loc.at[2 * CHUNKS + 2]))
    local.append(pltpu.make_async_copy(we, w_e.at[r], loc.at[2 * CHUNKS + 3]))
    local.append(pltpu.make_async_copy(wd, w_d.at[r], loc.at[2 * CHUNKS + 4]))
    for cp in local:
        cp.start()

    for c in range(CHUNKS):
        for q in range(4):
            x_t[c, q // 2, q % 2, 1, 3] = jnp.zeros((16, PAIR), BF16)
            res[c, q // 2, q % 2, 1, 3] = jnp.zeros((16, PAIR), BF16)
    barrier = pltpu.get_barrier_semaphore()
    partners = [far, other_core, twin] + [zpeer(k) for k in (1, 2, 3)]
    partners += [chip((y + k) % 4, x) for k in (1, 2, 3)] + [chip(y, (x + k) % 4) for k in (1, 2, 3)]
    for dev in partners:
        pl.semaphore_signal(barrier, inc=1, device_id=dev, device_id_type=MESH)
    for c in range(CHUNKS):
        for q in range(4):
            feat[c, q, ROWS:] = jnp.zeros((16, 256), BF16)
            pg[c, q, ROWS:] = jnp.zeros((16, 256), BF16)
            keep[c, q, ROWS:] = jnp.zeros((16, 128), F32)
    ids_cp.wait()
    keep_row = (ids[...] != BEGIN_TOKEN).astype(F32)
    mask[0] = jnp.broadcast_to(keep_row, mask.shape[1:]).astype(BF16)
    for cp in local:
        cp.wait()
    pl.semaphore_wait(barrier, len(partners))

    sends, pending, step = [], {}, {}

    def under(when, action):
        if when is None:
            action()
        else:
            pl.when(when)(action)

    def go(cp, when=None, arrives=None):
        under(when, cp.start)
        sends.append((cp, when))
        pending[len(sends)] = (cp, arrives)
        return len(sends)

    def got(*entries):
        for entry in entries:
            cp, arrives = pending.pop(entry)
            under(arrives, cp.wait_recv)

    def finish():
        got(*list(pending))
        for cp, when in sends:
            under(when, cp.wait_send)

    def both(a, b):
        return b if a is None else jnp.logical_and(a, b)

    def spread_first(buf, c, send, recv, rows=None):
        out = []
        for k in (1, 2, 3):
            xx, yy = (x + k) % 4, (y + k) % 4
            for u, dev, source in (
                (0, chip(y, xx), has_tile(y, (x + 4 - k) % 4)),
                (1, chip(yy, x), has_tile((y + 4 - k) % 4, x)),
            ):
                part = buf.at[c, y // 2, u, y % 2, x]
                lead = rows if u == 0 else None
                out.append(
                    go(remote(part, part, send.at[0, c, u, k - 1], recv.at[0, c, u, k - 1], dev),
                       both(lead, owns), both(lead, source))
                )
        return out

    def spread_second(buf, c, send, recv, rows=None):
        out = []
        for k in (1, 2, 3):
            xx, yy = (x + k) % 4, (y + k) % 4
            part = buf.at[c, y // 2, 0, y % 2]
            out.append(
                go(remote(part, part, send.at[1, c, 0, k - 1], recv.at[1, c, 0, k - 1], chip(yy, x)),
                   rows, None if rows is None else (y + 4 - k) % 4 >= 2)
            )
            part = buf.at[c, pl.ds(0, 2), 1, pl.ds(0, 2), x]
            out.append(go(remote(part, part, send.at[1, c, 1, k - 1], recv.at[1, c, 1, k - 1], chip(y, xx))))
        return out

    low = y >= 2
    tile = 4 * (y % 2) + x
    for c in range(CHUNKS):
        entries = []
        for k in (1, 2, 3):
            q = 4 - k
            there = pl.ds(pl.multiple_of(((p + k) % 4) * PAIR, 128), PAIR)
            when = both(low if q >= 2 else jnp.logical_not(low), owns)
            src = taps.at[lax.min(TILES * c + tile, taps.shape[0] - 1), :, there]
            dst = x_t.at[c, q // 2, q % 2, y % 2, x]
            entries.append(go(remote(src, dst, xz_s.at[c, k - 1], xz_r.at[c, q - 1], zpeer(k)), when, when))
        step["xz", c] = entries
    mask_cp = [go(remote(mask.at[0], mask.at[4 - k], mk_s.at[k - 1], mk_r.at[3 - k], zpeer(k))) for k in (1, 2, 3)]

    def taps_first(c):
        got(*step["xz", c])
        step["xa", c] = spread_first(x_t, c, xy_s, xy_r, low)
        if c == CHUNKS - 1:
            step["we"] = go(remote(we, w_e.at[r], one_s.at[0], one_r.at[0], twin))
            step["wd"] = go(remote(wd, w_d.at[r], one_s.at[1], one_r.at[1], twin))

    def taps_second(c):
        got(*step["xa", c])
        step["xb", c] = spread_second(x_t, c, xy_s, xy_r, low)

    def norms_first(c):
        got(step["wd"])
        w_sq = jnp.square(w_d[...].astype(F32)).reshape(PAIR, 256)
        nsq[0] = jnp.broadcast_to(jnp.sum(w_sq, axis=0, keepdims=True), (8, 256))
        step["ns"] = [
            go(remote(nsq.at[0], nsq.at[4 - k], ns_s.at[k - 1], ns_r.at[3 - k], zpeer(k))) for k in (1, 2, 3)
        ]
        got(*mask_cp)
        unit = jnp.full((16, 128), 1.0 / 16.0, BF16)
        for q in range(4):
            column = lax.dot_general(mask[q], unit, (((0,), (0,)), ((), ())), preferred_element_type=F32)
            for c in range(CHUNKS):
                keep[c, q, :ROWS] = column[c * ROWS:(c + 1) * ROWS]

    def norms_second(c):
        got(*step["ns"])
        cnorm[...] = jnp.sqrt(nsq[0] + nsq[1] + nsq[2] + nsq[3] + 1e-06)
        step["cn"] = go(remote(cnorm, cnorm_o, one_s.at[2], one_r.at[2], other_core))

    def z_group(sem, src, dst, c):
        return [
            go(remote(src(k), dst(4 - k), zg_s.at[sem, c, k - 1], zg_r.at[sem, c, 3 - k], zpeer(k)))
            for k in (1, 2, 3)
        ]

    def cross(c, sem, full, got_ref):
        return go(
            remote(full.at[c, :, real, theirs], got_ref.at[c], co_s.at[sem, c], co_r.at[sem, c], other_core)
        )

    def cross_half(c, sem, full):
        block = full.at[c, :, real, mine]
        return go(remote(block, block, co_s.at[sem, c], co_r.at[sem, c], other_core))

    def rows_of(ref, c):
        return ref[c].reshape(4 * PADDED, ref.shape[-1])

    def pre_dot(c):
        got(*step["xb", c])
        if c == 0:
            got(step["we"])
        part = jnp.dot(rows_of(x_t, c), w_e[...].reshape(PAIR, 256), preferred_element_type=F32)
        pre_f[c] = part.reshape(4, PADDED, 256)
        step["pc", c] = cross(c, 0, pre_f, pre_x)

    def pre_sum(c):
        got(step["pc", c])
        for q in (1, 2, 3):
            pre_s[c, q - 1] = (pre_f[c, q, :ROWS, mine] + pre_x[c, q]).astype(BF16)
        step["pz", c] = z_group(0, lambda k: pre_s.at[c, k - 1], lambda q: pre_r.at[c, q - 1], c)
        pre_own[c] = pre_f[c, 0, :ROWS, mine] + pre_x[c, 0]

    def pre_act(c):
        got(*step["pz", c])
        preact = pre_own[c] + bias[...]
        for q in range(3):
            preact = preact + pre_r[c, q].astype(F32)
        pre_own[c] = preact
        feat[c, 0, :ROWS, mine] = smooth_relu(preact).astype(BF16)
        step["fz", c] = z_group(1, lambda k: feat.at[c, 0, real, mine], lambda q: feat.at[c, q, real, mine], c)

    def feat_cross(c):
        got(*step["fz", c])
        step["fc", c] = cross_half(c, 1, feat)

    def reb_dot(c):
        got(step["fc", c])
        part = lax.dot_general(
            rows_of(feat, c), w_d[...].reshape(PAIR, 256), (((1,), (1,)), ((), ())), preferred_element_type=F32
        )
        reb[c] = part.astype(BF16).reshape(2, 2, 2, 4, 16, PAIR)
        step["ra", c] = []
        for k in (1, 2, 3):
            xx, yy = (x + k) % 4, (y + k) % 4
            step["ra", c].append(go(remote(
                reb.at[c, pl.ds(0, 2), 0, pl.ds(0, 2), xx], row_r.at[c, k - 1],
                rr_s.at[0, c, 0, k - 1], rr_r.at[0, c, 0, k - 1], chip(y, xx))))
            step["ra", c].append(go(remote(
                reb.at[c, yy // 2, 1, yy % 2], col_r.at[c, k - 1],
                rr_s.at[0, c, 1, k - 1], rr_r.at[0, c, 1, k - 1], chip(yy, x))))

    def reb_mid(c):
        got(*step["ra", c])
        total = reb[c, :, 0, :, x].astype(F32)
        for k in range(3):
            total = total + row_r[c, k].astype(F32)
        row_s[c] = total.astype(BF16)
        own_s[c, 0] = row_s[c, y // 2, y % 2]
        total = reb[c, y // 2, 1, y % 2].astype(F32)
        for k in range(3):
            total = total + col_r[c, k].astype(F32)
        col_s[c] = total.astype(BF16)
        own_s[c, 1] = col_s[c, x]
        step["rb", c] = []
        for k in (1, 2, 3):
            xx, yy = (x + k) % 4, (y + k) % 4
            step["rb", c].append(go(remote(
                row_s.at[c, yy // 2, yy % 2], end_r.at[c, k - 1, 0],
                rr_s.at[1, c, 0, k - 1], rr_r.at[1, c, 0, k - 1], chip(yy, x)), has_tile(yy, x), owns))
            step["rb", c].append(go(remote(
                col_s.at[c, xx], end_r.at[c, k - 1, 1],
                rr_s.at[1, c, 1, k - 1], rr_r.at[1, c, 1, k - 1], chip(y, xx)), has_tile(y, xx), owns))

    def reb_sum(c):
        got(*step["rb", c])

        @pl.when(owns)
        def _():
            total = own_s[c].astype(F32)
            for k in range(3):
                total = total + end_r[c, k].astype(F32)
            zs[c] = total
            zb[c] = total.astype(BF16)

        step["zh", c] = go(remote(zb.at[c], zr.at[c], zh_s.at[c], zh_r.at[c], far), owns, owns)

    def residue(c):
        got(step["zh", c])

        @pl.when(owns)
        def _():
            rebuilt = zs[c] + zr[c].astype(F32) + dbias[...].reshape(1, 1, PAIR)
            diff = rebuilt - x_t[c, y // 2, :, y % 2, x].astype(F32)
            spot = pl.ds(pl.multiple_of(16 * tile, 16), 16)
            weight = loss_scale * keep[c, pl.ds(2 * (y // 2), 2), spot][:, :, :1]
            res[c, y // 2, :, y % 2, x] = (weight * diff).astype(BF16)

        step["sa", c] = spread_first(res, c, rs_s, rs_r)

    def residue_second(c):
        got(*step["sa", c])
        step["sb", c] = spread_second(res, c, rs_s, rs_r)

    def grad_dot(c):
        got(*step["sb", c])
        part = jnp.dot(rows_of(res, c), w_d[...].reshape(PAIR, 256), preferred_element_type=F32)
        g_f[c] = part.reshape(4, PADDED, 256)
        step["gc", c] = cross(c, 2, g_f, g_x)

    def grad_sum(c):
        got(step["gc", c])
        for q in (1, 2, 3):
            g_s[c, q - 1] = (g_f[c, q, :ROWS, mine] + g_x[c, q]).astype(BF16)
        step["gz", c] = z_group(2, lambda k: g_s.at[c, k - 1], lambda q: g_r.at[c, q - 1], c)
        g_own[c] = g_f[c, 0, :ROWS, mine] + g_x[c, 0]

    def grad_pre(c):
        if c == 0:
            got(step["cn"])
        got(*step["gz", c])
        norm_total = cnorm[0:1, mine] + cnorm_o[0:1, mine]
        grads = g_own[c] + loss_scale * SPARSITY * keep[c, 0, :ROWS] * norm_total
        for q in range(3):
            grads = grads + g_r[c, q].astype(F32)
        pg[c, 0, :ROWS, mine] = (grads * relu_slope(pre_own[c])).astype(BF16)
        step["qz", c] = z_group(3, lambda k: pg.at[c, 0, real, mine], lambda q: pg.at[c, q, real, mine], c)

    def grad_cross(c):
        got(*step["qz", c])
        step["qc", c] = cross_half(c, 3, pg)

    def dec_grad(c):
        f = rows_of(feat, c)
        active = jnp.sum(rows_of(keep, c)[:, :1] * f.astype(F32), axis=0, keepdims=True)
        penalty = loss_scale * SPARSITY * active / cnorm[0:1, :]
        total = w_d[...].reshape(PAIR, 256).astype(F32) * penalty + lax.dot_general(
            rows_of(res, c), f, (((0,), (0,)), ((), ())), preferred_element_type=F32
        )
        total = total.reshape(2, PAIR // 2, 256)
        dwd[...] = total if c == 0 else dwd[...] + total
        if c == CHUNKS - 1:
            dwd_s[...] = dwd[1 - r].astype(BF16)
            step["dwd"] = go(remote(dwd_s, dwd_r, one_s.at[3], one_r.at[3], twin))

    def enc_grad(c):
        got(step["qc", c])
        total = lax.dot_general(
            rows_of(x_t, c), rows_of(pg, c), (((0,), (0,)), ((), ())), preferred_element_type=F32
        ).reshape(2, PAIR // 2, 256)
        dwe[...] = total if c == 0 else dwe[...] + total
        if c == CHUNKS - 1:
            dwe_s[...] = dwe[1 - r].astype(BF16)
            step["dwe"] = go(remote(dwe_s, dwe_r, one_s.at[4], one_r.at[4], twin))

    stages = {
        "taps_first": taps_first,
        "taps_second": taps_second,
        "pre_dot": pre_dot,
        "pre_sum": pre_sum,
        "pre_act": pre_act,
        "feat_cross": feat_cross,
        "reb_dot": reb_dot,
        "reb_mid": reb_mid,
        "reb_sum": reb_sum,
        "residue": residue,
        "residue_second": residue_second,
        "grad_dot": grad_dot,
        "grad_sum": grad_sum,
        "grad_pre": grad_pre,
        "grad_cross": grad_cross,
        "enc_grad": enc_grad,
        "dec_grad": dec_grad,
        "norms_first": norms_first,
        "norms_second": norms_second,
    }
    for stage, c in ORDER:
        stages[stage](c)
    got(step["dwd"])
    dec_out[...] = (dwd[r] + dwd_r[...].astype(F32)).astype(BF16)
    got(step["dwe"])
    enc_out[...] = (dwe[r] + dwe_r[...].astype(F32)).astype(BF16)
    finish()


def local(taps, token_ids, enc_weight, enc_bias, dec_weight, dec_bias):
    tokens_dev = taps.shape[1]
    loss_scale = 1.0 / math.sqrt(tokens_dev * lax.axis_size("token"))
    c = CHUNKS
    dma = pltpu.SemaphoreType.DMA
    vmem = pltpu.VMEM
    tiles = (c, 2, 2, 2, 4, 16, PAIR)
    scratch = [
        vmem((1, tokens_dev), jnp.int32), vmem((1, 128), F32), vmem((1, PAIR), F32),
        vmem(tiles, BF16),
        vmem((2, 448, 256), BF16), vmem((2, 448, 256), BF16),
        vmem((4, 16, 224), BF16), vmem((c, 4, PADDED, 128), F32),
        vmem((4, 8, 256), F32), vmem((8, 256), F32), vmem((8, 256), F32),
        vmem((c, 4, PADDED, 256), F32), vmem((c, 4, ROWS, 128), F32),
        vmem((c, 3, ROWS, 128), BF16), vmem((c, 3, ROWS, 128), BF16), vmem((c, ROWS, 128), F32),
        vmem((c, 4, PADDED, 256), BF16),
        vmem(tiles, BF16),
        vmem((c, 3, 2, 2, 16, PAIR), BF16), vmem((c, 3, 4, 16, PAIR), BF16),
        vmem((c, 2, 2, 16, PAIR), BF16), vmem((c, 4, 16, PAIR), BF16),
        vmem((c, 2, 16, PAIR), BF16), vmem((c, 3, 2, 16, PAIR), BF16),
        vmem((c, 2, 16, PAIR), F32), vmem((c, 2, 16, PAIR), BF16), vmem((c, 2, 16, PAIR), BF16),
        vmem(tiles, BF16),
        vmem((c, 4, PADDED, 256), F32), vmem((c, 4, ROWS, 128), F32),
        vmem((c, 3, ROWS, 128), BF16), vmem((c, 3, ROWS, 128), BF16), vmem((c, ROWS, 128), F32),
        vmem((c, 4, PADDED, 256), BF16),
        vmem((2, 448, 256), F32), vmem((448, 256), BF16), vmem((448, 256), BF16),
        vmem((2, 448, 256), F32), vmem((448, 256), BF16), vmem((448, 256), BF16),
        dma((2 * c + 5,)),
        dma((c, 3)), dma((c, 3)), dma((2, c, 2, 3)), dma((2, c, 2, 3)),
        dma((3,)), dma((3,)), dma((3,)), dma((3,)),
        dma((5,)), dma((5,)),
        dma((4, c)), dma((4, c)), dma((4, c, 3)), dma((4, c, 3)),
        dma((2, c, 2, 3)), dma((2, c, 2, 3)), dma((c,)), dma((c,)), dma((2, c, 2, 3)), dma((2, c, 2, 3)),
    ]
    any_spec = pl.BlockSpec(memory_space=pl.ANY)
    vmem_spec = pl.BlockSpec(memory_space=pltpu.VMEM)
    enc_grad, dec_grad = pl.pallas_call(
        functools.partial(kernel, loss_scale),
        out_shape=(jax.ShapeDtypeStruct((448, 256), BF16), jax.ShapeDtypeStruct((448, 256), BF16)),
        in_specs=[any_spec] * 6,
        out_specs=(vmem_spec, vmem_spec),
        scratch_shapes=scratch,
        compiler_params=pltpu.CompilerParams(
            collective_id=0, has_side_effects=True, vmem_limit_bytes=60 * 1024 * 1024
        ),
        name="crosscoder",
    )(taps.reshape(tokens_dev // 16, 16, taps.shape[2]), token_ids[None, :], enc_weight[0], enc_bias[None, :], dec_weight[0], dec_bias)
    return enc_grad[None], dec_grad[None]


def solution(mesh):
    placed = (
        P("layer", "token", None),
        P("token"),
        P("layer", "token", "latent"),
        P("latent"),
        P("layer", "token", "latent"),
        P("layer", None),
    )
    return jax.shard_map(
        local,
        mesh=mesh,
        in_specs=placed,
        out_specs=(P("layer", "token", "latent"), P("layer", "token", "latent")),
        check_vma=False,
    )
```

```python
import functools
import math

import jax
import jax.numpy as jnp
from jax import lax
from jax.experimental import pallas as pl
from jax.experimental.pallas import tpu as pltpu
from jax.sharding import PartitionSpec as P

KNEE_WIDTH = 0.5
SPARSITY = 0.5
BEGIN_TOKEN = 2
MESH = pl.DeviceIdType.MESH
F32 = jnp.float32
BF16 = jnp.bfloat16

CHUNKS = 2
ROWS = 112
PADDED = 128
TILES = 7
PAIR = 896

GROUPS = (
    ("taps_first",), ("taps_second",), ("pre_dot", "pre_sum"), ("pre_act",), ("feat_cross", "reb_dot"), ("reb_mid",),
    ("reb_sum",), ("residue",), ("residue_second",), ("grad_dot", "grad_sum"), ("grad_pre",), ("grad_cross", "enc_grad"),
)
LAG = 1
ORDER = [
    (stage, c)
    for _, c, g in sorted((g + LAG * c, c, g) for g in range(len(GROUPS)) for c in range(CHUNKS))
    for stage in GROUPS[g]
]
for after, extra in (
    (("grad_pre", CHUNKS - 1), [("dec_grad", c) for c in range(CHUNKS)]),
    (("reb_dot", 0), [("norms_first", 0)]),
    (("reb_sum", 0), [("norms_second", 0)]),
):
    spot = ORDER.index(after) + 1
    ORDER[spot:spot] = extra


def smooth_relu(preact):
    positive = jnp.maximum(preact, 0.0)
    return jnp.where(
        positive < KNEE_WIDTH, positive * positive / (2.0 * KNEE_WIDTH), positive - 0.5 * KNEE_WIDTH
    )


def relu_slope(preact):
    return jnp.clip(preact / KNEE_WIDTH, 0.0, 1.0)


def kernel(loss_scale, taps, ids_in, we, eb, wd, db, enc_out, dec_out,
           ids, bias, dbias, x_t, w_e, w_d, mask, keep, nsq, cnorm, cnorm_o,
           pre_f, pre_o, pre_x, pre_s, pre_r, pre_own, feat, reb, row_r, col_r, row_s, col_s, own_s, end_r,
           zs, zb, zr, res, g_f, g_o, g_x, g_s, g_r, g_own, pg, dwd, dwd_s, dwd_r, dwe, dwe_s, dwe_r,
           loc, xz_s, xz_r, xy_s, xy_r, mk_s, mk_r, ns_s, ns_r, one_s, one_r,
           co_s, co_r, zg_s, zg_r, rr_s, rr_r, zh_s, zh_r, rs_s, rs_r):
    layer = lax.axis_index("layer")
    n = lax.axis_index("latent")
    m = lax.axis_index("token")
    h = n // 16
    y = (n // 4) % 4
    x = n % 4
    p = m // 2
    r = m % 2

    other_core = (1 - layer, n, m)
    twin = (layer, n, 2 * p + 1 - r)
    far = (layer, (1 - h) * 16 + n % 16, m)

    def zpeer(k):
        return (layer, n, 2 * ((p + k) % 4) + r)

    def chip(yy, xx):
        return (layer, h * 16 + yy * 4 + xx, m)

    def half(i):
        return pl.ds(pl.multiple_of(i * 128, 128), 128)

    mine = half(layer)
    cols = pl.ds(pl.multiple_of(p * PAIR, 128), PAIR)
    real = pl.ds(0, ROWS)

    def has_tile(yy, xx):
        return jnp.logical_not(jnp.logical_and(yy % 2 == 1, xx == 3))

    owns = has_tile(y, x)

    def remote(src, dst, send, recv, dev):
        return pltpu.make_async_remote_copy(
            src_ref=src, dst_ref=dst, send_sem=send, recv_sem=recv, device_id=dev, device_id_type=MESH
        )

    local = []
    for c in range(CHUNKS):
        local.append(pltpu.make_async_copy(taps.at[pl.ds(TILES * c, 4), :, cols], x_t.at[c, 0, 0, 0], loc.at[2 * c]))
        local.append(
            pltpu.make_async_copy(
                taps.at[pl.ds(TILES * c + 4, 3), :, cols], x_t.at[c, 0, 0, 1, pl.ds(0, 3)], loc.at[2 * c + 1]
            )
        )
    ids_cp = pltpu.make_async_copy(ids_in, ids, loc.at[2 * CHUNKS])
    ids_cp.start()
    local.append(pltpu.make_async_copy(eb.at[:, mine], bias, loc.at[2 * CHUNKS + 1]))
    local.append(pltpu.make_async_copy(db.at[:, cols], dbias, loc.at[2 * CHUNKS + 2]))
    local.append(pltpu.make_async_copy(we, w_e.at[r], loc.at[2 * CHUNKS + 3]))
    local.append(pltpu.make_async_copy(wd, w_d.at[r], loc.at[2 * CHUNKS + 4]))
    for cp in local:
        cp.start()

    for c in range(CHUNKS):
        for q in range(4):
            x_t[c, q // 2, q % 2, 1, 3] = jnp.zeros((16, PAIR), BF16)
            res[c, q // 2, q % 2, 1, 3] = jnp.zeros((16, PAIR), BF16)
    barrier = pltpu.get_barrier_semaphore()
    partners = [far, other_core, twin] + [zpeer(k) for k in (1, 2, 3)]
    partners += [chip((y + k) % 4, x) for k in (1, 2, 3)] + [chip(y, (x + k) % 4) for k in (1, 2, 3)]
    for dev in partners:
        pl.semaphore_signal(barrier, inc=1, device_id=dev, device_id_type=MESH)
    for c in range(CHUNKS):
        for q in range(4):
            for i in range(2):
                feat[c, i, q, ROWS:] = jnp.zeros((16, 128), BF16)
                pg[c, i, q, ROWS:] = jnp.zeros((16, 128), BF16)
            keep[c, q, ROWS:] = jnp.zeros((16, 128), F32)
    ids_cp.wait()
    keep_row = (ids[...] != BEGIN_TOKEN).astype(F32)
    mask[0] = jnp.broadcast_to(keep_row, mask.shape[1:]).astype(BF16)
    for cp in local:
        cp.wait()
    pl.semaphore_wait(barrier, len(partners))

    sends, pending, step = [], {}, {}

    def under(when, action):
        if when is None:
            action()
        else:
            pl.when(when)(action)

    def go(cp, when=None, arrives=None):
        under(when, cp.start)
        sends.append((cp, when))
        pending[len(sends)] = (cp, arrives)
        return len(sends)

    def got(*entries):
        for entry in entries:
            cp, arrives = pending.pop(entry)
            under(arrives, cp.wait_recv)

    def finish():
        got(*list(pending))
        for cp, when in sends:
            under(when, cp.wait_send)

    def both(a, b):
        return b if a is None else jnp.logical_and(a, b)

    def spread_first(buf, c, send, recv, rows=None):
        out = []
        for k in (1, 2, 3):
            xx, yy = (x + k) % 4, (y + k) % 4
            for u, dev, source in (
                (0, chip(y, xx), has_tile(y, (x + 4 - k) % 4)),
                (1, chip(yy, x), has_tile((y + 4 - k) % 4, x)),
            ):
                part = buf.at[c, y // 2, u, y % 2, x]
                lead = rows if u == 0 else None
                out.append(
                    go(remote(part, part, send.at[0, c, u, k - 1], recv.at[0, c, u, k - 1], dev),
                       both(lead, owns), both(lead, source))
                )
        return out

    def spread_second(buf, c, send, recv, rows=None):
        out = []
        for k in (1, 2, 3):
            xx, yy = (x + k) % 4, (y + k) % 4
            part = buf.at[c, y // 2, 0, y % 2]
            out.append(
                go(remote(part, part, send.at[1, c, 0, k - 1], recv.at[1, c, 0, k - 1], chip(yy, x)),
                   rows, None if rows is None else (y + 4 - k) % 4 >= 2)
            )
            part = buf.at[c, pl.ds(0, 2), 1, pl.ds(0, 2), x]
            out.append(go(remote(part, part, send.at[1, c, 1, k - 1], recv.at[1, c, 1, k - 1], chip(y, xx))))
        return out

    low = y >= 2
    tile = 4 * (y % 2) + x
    for c in range(CHUNKS):
        entries = []
        for k in (1, 2, 3):
            q = 4 - k
            there = pl.ds(pl.multiple_of(((p + k) % 4) * PAIR, 128), PAIR)
            when = both(low if q >= 2 else jnp.logical_not(low), owns)
            src = taps.at[lax.min(TILES * c + tile, taps.shape[0] - 1), :, there]
            dst = x_t.at[c, q // 2, q % 2, y % 2, x]
            entries.append(go(remote(src, dst, xz_s.at[c, k - 1], xz_r.at[c, q - 1], zpeer(k)), when, when))
        step["xz", c] = entries
    mask_cp = [go(remote(mask.at[0], mask.at[4 - k], mk_s.at[k - 1], mk_r.at[3 - k], zpeer(k))) for k in (1, 2, 3)]

    def taps_first(c):
        got(*step["xz", c])
        step["xa", c] = spread_first(x_t, c, xy_s, xy_r, low)
        if c == CHUNKS - 1:
            step["we"] = go(remote(we, w_e.at[r], one_s.at[0], one_r.at[0], twin))

    def taps_second(c):
        got(*step["xa", c])
        step["xb", c] = spread_second(x_t, c, xy_s, xy_r, low)

    def norms_first(c):
        w_sq = jnp.square(w_d[...].astype(F32)).reshape(PAIR, 256)
        nsq[0] = jnp.broadcast_to(jnp.sum(w_sq, axis=0, keepdims=True), (8, 256))
        step["ns"] = [
            go(remote(nsq.at[0], nsq.at[4 - k], ns_s.at[k - 1], ns_r.at[3 - k], zpeer(k))) for k in (1, 2, 3)
        ]
        got(*mask_cp)
        unit = jnp.full((16, 128), 1.0 / 16.0, BF16)
        for q in range(4):
            column = lax.dot_general(mask[q], unit, (((0,), (0,)), ((), ())), preferred_element_type=F32)
            for c in range(CHUNKS):
                keep[c, q, :ROWS] = column[c * ROWS:(c + 1) * ROWS]

    def norms_second(c):
        got(*step["ns"])
        cnorm[...] = jnp.sqrt(nsq[0] + nsq[1] + nsq[2] + nsq[3] + 1e-06)
        step["cn"] = go(remote(cnorm, cnorm_o, one_s.at[2], one_r.at[2], other_core))

    def z_group(sem, src, dst, c):
        return [
            go(remote(src(k), dst(4 - k), zg_s.at[sem, c, k - 1], zg_r.at[sem, c, 3 - k], zpeer(k)))
            for k in (1, 2, 3)
        ]

    def cross(c, sem, part, own_ref, out_ref, got_ref):
        part = part.reshape(4, PADDED, 256)[:, :ROWS]
        is_low = layer == 0
        own_ref[c] = jnp.where(is_low, part[:, :, :128], part[:, :, 128:])
        out_ref[c] = jnp.where(is_low, part[:, :, 128:], part[:, :, :128]).astype(BF16)
        return go(remote(out_ref.at[c], got_ref.at[c], co_s.at[sem, c], co_r.at[sem, c], other_core))

    def cross_half(c, sem, full):
        block = full.at[c, layer, :, real]
        return go(remote(block, block, co_s.at[sem, c], co_r.at[sem, c], other_core))

    def rows_of(ref, c):
        return ref[c].reshape(4 * PADDED, ref.shape[-1])

    def wide(ref, c):
        return jnp.concatenate([ref[c, i].reshape(4 * PADDED, 128) for i in range(2)], axis=1)

    def pre_dot(c):
        got(*step["xb", c])
        if c == 0:
            got(step["we"])
        part = jnp.dot(rows_of(x_t, c), w_e[...].reshape(PAIR, 256), preferred_element_type=F32)
        step["pc", c] = cross(c, 0, part, pre_f, pre_o, pre_x)

    def pre_sum(c):
        got(step["pc", c])
        for q in (1, 2, 3):
            pre_s[c, q - 1] = (pre_f[c, q] + pre_x[c, q].astype(F32)).astype(BF16)
        step["pz", c] = z_group(0, lambda k: pre_s.at[c, k - 1], lambda q: pre_r.at[c, q - 1], c)
        if c == 0:
            step["wd"] = go(remote(wd, w_d.at[r], one_s.at[1], one_r.at[1], twin))
        pre_own[c] = pre_f[c, 0] + pre_x[c, 0].astype(F32)

    def pre_act(c):
        got(*step["pz", c])
        preact = pre_own[c] + bias[...]
        for q in range(3):
            preact = preact + pre_r[c, q].astype(F32)
        pre_own[c] = preact
        feat[c, layer, 0, :ROWS] = smooth_relu(preact).astype(BF16)
        step["fz", c] = z_group(1, lambda k: feat.at[c, layer, 0, real], lambda q: feat.at[c, layer, q, real], c)

    def feat_cross(c):
        got(*step["fz", c])
        step["fc", c] = cross_half(c, 1, feat)

    def reb_dot(c):
        got(step["fc", c])
        if c == 0:
            got(step["wd"])
        part = lax.dot_general(
            wide(feat, c), w_d[...].reshape(PAIR, 256), (((1,), (1,)), ((), ())), preferred_element_type=F32
        )
        reb[c] = part.astype(BF16).reshape(2, 2, 2, 4, 16, PAIR)
        step["ra", c] = []
        for k in (1, 2, 3):
            xx, yy = (x + k) % 4, (y + k) % 4
            step["ra", c].append(go(remote(
                reb.at[c, pl.ds(0, 2), 0, pl.ds(0, 2), xx], row_r.at[c, k - 1],
                rr_s.at[0, c, 0, k - 1], rr_r.at[0, c, 0, k - 1], chip(y, xx))))
            step["ra", c].append(go(remote(
                reb.at[c, yy // 2, 1, yy % 2], col_r.at[c, k - 1],
                rr_s.at[0, c, 1, k - 1], rr_r.at[0, c, 1, k - 1], chip(yy, x))))

    def reb_mid(c):
        got(*step["ra", c])
        total = reb[c, :, 0, :, x].astype(F32)
        for k in range(3):
            total = total + row_r[c, k].astype(F32)
        row_s[c] = total.astype(BF16)
        own_s[c, 0] = row_s[c, y // 2, y % 2]
        total = reb[c, y // 2, 1, y % 2].astype(F32)
        for k in range(3):
            total = total + col_r[c, k].astype(F32)
        col_s[c] = total.astype(BF16)
        own_s[c, 1] = col_s[c, x]
        step["rb", c] = []
        for k in (1, 2, 3):
            xx, yy = (x + k) % 4, (y + k) % 4
            step["rb", c].append(go(remote(
                row_s.at[c, yy // 2, yy % 2], end_r.at[c, k - 1, 0],
                rr_s.at[1, c, 0, k - 1], rr_r.at[1, c, 0, k - 1], chip(yy, x)), has_tile(yy, x), owns))
            step["rb", c].append(go(remote(
                col_s.at[c, xx], end_r.at[c, k - 1, 1],
                rr_s.at[1, c, 1, k - 1], rr_r.at[1, c, 1, k - 1], chip(y, xx)), has_tile(y, xx), owns))

    def reb_sum(c):
        got(*step["rb", c])

        @pl.when(owns)
        def _():
            total = own_s[c].astype(F32)
            for k in range(3):
                total = total + end_r[c, k].astype(F32)
            zs[c] = total
            zb[c] = total.astype(BF16)

        step["zh", c] = go(remote(zb.at[c], zr.at[c], zh_s.at[c], zh_r.at[c], far), owns, owns)

    def residue(c):
        got(step["zh", c])

        @pl.when(owns)
        def _():
            rebuilt = zs[c] + zr[c].astype(F32) + dbias[...].reshape(1, 1, PAIR)
            diff = rebuilt - x_t[c, y // 2, :, y % 2, x].astype(F32)
            spot = pl.ds(pl.multiple_of(16 * tile, 16), 16)
            weight = loss_scale * keep[c, pl.ds(2 * (y // 2), 2), spot][:, :, :1]
            res[c, y // 2, :, y % 2, x] = (weight * diff).astype(BF16)

        step["sa", c] = spread_first(res, c, rs_s, rs_r)

    def residue_second(c):
        got(*step["sa", c])
        step["sb", c] = spread_second(res, c, rs_s, rs_r)

    def grad_dot(c):
        got(*step["sb", c])
        part = jnp.dot(rows_of(res, c), w_d[...].reshape(PAIR, 256), preferred_element_type=F32)
        step["gc", c] = cross(c, 2, part, g_f, g_o, g_x)

    def grad_sum(c):
        got(step["gc", c])
        for q in (1, 2, 3):
            g_s[c, q - 1] = (g_f[c, q] + g_x[c, q].astype(F32)).astype(BF16)
        step["gz", c] = z_group(2, lambda k: g_s.at[c, k - 1], lambda q: g_r.at[c, q - 1], c)
        g_own[c] = g_f[c, 0] + g_x[c, 0].astype(F32)

    def grad_pre(c):
        if c == 0:
            got(step["cn"])
        got(*step["gz", c])
        norm_total = cnorm[0:1, mine] + cnorm_o[0:1, mine]
        grads = g_own[c] + loss_scale * SPARSITY * keep[c, 0, :ROWS] * norm_total
        for q in range(3):
            grads = grads + g_r[c, q].astype(F32)
        pg[c, layer, 0, :ROWS] = (grads * relu_slope(pre_own[c])).astype(BF16)
        step["qz", c] = z_group(3, lambda k: pg.at[c, layer, 0, real], lambda q: pg.at[c, layer, q, real], c)

    def grad_cross(c):
        got(*step["qz", c])
        step["qc", c] = cross_half(c, 3, pg)

    def dec_grad(c):
        f = wide(feat, c)
        active = jnp.sum(rows_of(keep, c)[:, :1] * f.astype(F32), axis=0, keepdims=True)
        penalty = loss_scale * SPARSITY * active / cnorm[0:1, :]
        total = w_d[...].reshape(PAIR, 256).astype(F32) * penalty + lax.dot_general(
            rows_of(res, c), f, (((0,), (0,)), ((), ())), preferred_element_type=F32
        )
        total = total.reshape(2, PAIR // 2, 256)
        dwd[...] = total if c == 0 else dwd[...] + total
        if c == CHUNKS - 1:
            dwd_s[...] = dwd[1 - r].astype(BF16)
            step["dwd"] = go(remote(dwd_s, dwd_r, one_s.at[3], one_r.at[3], twin))

    def enc_grad(c):
        got(step["qc", c])
        total = lax.dot_general(
            rows_of(x_t, c), wide(pg, c), (((0,), (0,)), ((), ())), preferred_element_type=F32
        ).reshape(2, PAIR // 2, 256)
        dwe[...] = total if c == 0 else dwe[...] + total
        if c == CHUNKS - 1:
            dwe_s[...] = dwe[1 - r].astype(BF16)
            step["dwe"] = go(remote(dwe_s, dwe_r, one_s.at[4], one_r.at[4], twin))

    stages = {
        "taps_first": taps_first,
        "taps_second": taps_second,
        "pre_dot": pre_dot,
        "pre_sum": pre_sum,
        "pre_act": pre_act,
        "feat_cross": feat_cross,
        "reb_dot": reb_dot,
        "reb_mid": reb_mid,
        "reb_sum": reb_sum,
        "residue": residue,
        "residue_second": residue_second,
        "grad_dot": grad_dot,
        "grad_sum": grad_sum,
        "grad_pre": grad_pre,
        "grad_cross": grad_cross,
        "enc_grad": enc_grad,
        "dec_grad": dec_grad,
        "norms_first": norms_first,
        "norms_second": norms_second,
    }
    for stage, c in ORDER:
        stages[stage](c)
    got(step["dwd"])
    dec_out[...] = (dwd[r] + dwd_r[...].astype(F32)).astype(BF16)
    got(step["dwe"])
    enc_out[...] = (dwe[r] + dwe_r[...].astype(F32)).astype(BF16)
    finish()


def local(taps, token_ids, enc_weight, enc_bias, dec_weight, dec_bias):
    tokens_dev = taps.shape[1]
    loss_scale = 1.0 / math.sqrt(tokens_dev * lax.axis_size("token"))
    c = CHUNKS
    dma = pltpu.SemaphoreType.DMA
    vmem = pltpu.VMEM
    tiles = (c, 2, 2, 2, 4, 16, PAIR)
    scratch = [
        vmem((1, tokens_dev), jnp.int32), vmem((1, 128), F32), vmem((1, PAIR), F32),
        vmem(tiles, BF16),
        vmem((2, 448, 256), BF16), vmem((2, 448, 256), BF16),
        vmem((4, 16, 224), BF16), vmem((c, 4, PADDED, 128), F32),
        vmem((4, 8, 256), F32), vmem((8, 256), F32), vmem((8, 256), F32),
        vmem((c, 4, ROWS, 128), F32), vmem((c, 4, ROWS, 128), BF16), vmem((c, 4, ROWS, 128), BF16),
        vmem((c, 3, ROWS, 128), BF16), vmem((c, 3, ROWS, 128), BF16), vmem((c, ROWS, 128), F32),
        vmem((c, 2, 4, PADDED, 128), BF16),
        vmem(tiles, BF16),
        vmem((c, 3, 2, 2, 16, PAIR), BF16), vmem((c, 3, 4, 16, PAIR), BF16),
        vmem((c, 2, 2, 16, PAIR), BF16), vmem((c, 4, 16, PAIR), BF16),
        vmem((c, 2, 16, PAIR), BF16), vmem((c, 3, 2, 16, PAIR), BF16),
        vmem((c, 2, 16, PAIR), F32), vmem((c, 2, 16, PAIR), BF16), vmem((c, 2, 16, PAIR), BF16),
        vmem(tiles, BF16),
        vmem((c, 4, ROWS, 128), F32), vmem((c, 4, ROWS, 128), BF16), vmem((c, 4, ROWS, 128), BF16),
        vmem((c, 3, ROWS, 128), BF16), vmem((c, 3, ROWS, 128), BF16), vmem((c, ROWS, 128), F32),
        vmem((c, 2, 4, PADDED, 128), BF16),
        vmem((2, 448, 256), F32), vmem((448, 256), BF16), vmem((448, 256), BF16),
        vmem((2, 448, 256), F32), vmem((448, 256), BF16), vmem((448, 256), BF16),
        dma((2 * c + 5,)),
        dma((c, 3)), dma((c, 3)), dma((2, c, 2, 3)), dma((2, c, 2, 3)),
        dma((3,)), dma((3,)), dma((3,)), dma((3,)),
        dma((5,)), dma((5,)),
        dma((4, c)), dma((4, c)), dma((4, c, 3)), dma((4, c, 3)),
        dma((2, c, 2, 3)), dma((2, c, 2, 3)), dma((c,)), dma((c,)), dma((2, c, 2, 3)), dma((2, c, 2, 3)),
    ]
    any_spec = pl.BlockSpec(memory_space=pl.ANY)
    vmem_spec = pl.BlockSpec(memory_space=pltpu.VMEM)
    enc_grad, dec_grad = pl.pallas_call(
        functools.partial(kernel, loss_scale),
        out_shape=(jax.ShapeDtypeStruct((448, 256), BF16), jax.ShapeDtypeStruct((448, 256), BF16)),
        in_specs=[any_spec] * 6,
        out_specs=(vmem_spec, vmem_spec),
        scratch_shapes=scratch,
        compiler_params=pltpu.CompilerParams(
            collective_id=0, has_side_effects=True, vmem_limit_bytes=60 * 1024 * 1024
        ),
        name="crosscoder",
    )(taps.reshape(tokens_dev // 16, 16, taps.shape[2]), token_ids[None, :], enc_weight[0], enc_bias[None, :], dec_weight[0], dec_bias)
    return enc_grad[None], dec_grad[None]


def solution(mesh):
    placed = (
        P("layer", "token", None),
        P("token"),
        P("layer", "token", "latent"),
        P("latent"),
        P("layer", "token", "latent"),
        P("layer", None),
    )
    return jax.shard_map(
        local,
        mesh=mesh,
        in_specs=placed,
        out_specs=(P("layer", "token", "latent"), P("layer", "token", "latent")),
        check_vma=False,
    )
```

```python
import functools
import math

import jax
import jax.numpy as jnp
from jax import lax
from jax.experimental import pallas as pl
from jax.experimental.pallas import tpu as pltpu
from jax.sharding import PartitionSpec as P

KNEE_WIDTH = 0.5
SPARSITY = 0.5
BEGIN_TOKEN = 2
MESH = pl.DeviceIdType.MESH
F32 = jnp.float32
BF16 = jnp.bfloat16

CHUNKS = 2
ROWS = 112
PADDED = 128
TILES = 7
PAIR = 896

GROUPS = (
    ("taps_first",),
    ("taps_second",),
    ("pre_dot", "pre_sum",),
    ("pre_act",),
    ("feat_cross",),
    ("reb_dot",),
    ("reb_mid",),
    ("reb_sum",),
    ("residue",),
    ("residue_second",),
    ("grad_dot", "grad_sum",),
    ("grad_pre",),
    ("grad_cross", "enc_grad",),
)
LAG = 1
ORDER = [
    (stage, c)
    for _, c, g in sorted((g + LAG * c, c, g) for g in range(len(GROUPS)) for c in range(CHUNKS))
    for stage in GROUPS[g]
]
for after, extra in (
    (("grad_pre", CHUNKS - 1), [("dec_grad", c) for c in range(CHUNKS)]),
    (("reb_dot", 0), [("norms_first", 0)]),
    (("reb_sum", 0), [("norms_second", 0)]),
):
    spot = ORDER.index(after) + 1
    ORDER[spot:spot] = extra


def smooth_relu(preact):
    positive = jnp.maximum(preact, 0.0)
    return jnp.where(
        positive < KNEE_WIDTH, positive * positive / (2.0 * KNEE_WIDTH), positive - 0.5 * KNEE_WIDTH
    )


def relu_slope(preact):
    return jnp.clip(preact / KNEE_WIDTH, 0.0, 1.0)


def kernel(loss_scale, taps, ids_in, we, eb, wd, db, enc_out, dec_out,
           ids, bias, dbias, x_t, w_e, w_d, mask, keep, nsq, cnorm, cnorm_o,
           pre_f, pre_o, pre_x, pre_s, pre_r, pre_own, feat, reb, row_r, col_r, row_s, col_s, own_s, end_r,
           zs, zb, zr, res, g_f, g_o, g_x, g_s, g_r, g_own, pg, dwd, dwd_s, dwd_r, dwe, dwe_s, dwe_r,
           loc, xz_s, xz_r, xy_s, xy_r, mk_s, mk_r, ns_s, ns_r, one_s, one_r,
           co_s, co_r, zg_s, zg_r, rr_s, rr_r, zh_s, zh_r, rs_s, rs_r):
    layer = lax.axis_index("layer")
    n = lax.axis_index("latent")
    m = lax.axis_index("token")
    h = n // 16
    y = (n // 4) % 4
    x = n % 4
    p = m // 2
    r = m % 2

    other_core = (1 - layer, n, m)
    twin = (layer, n, 2 * p + 1 - r)
    far = (layer, (1 - h) * 16 + n % 16, m)

    def zpeer(k):
        return (layer, n, 2 * ((p + k) % 4) + r)

    def chip(yy, xx):
        return (layer, h * 16 + yy * 4 + xx, m)

    def half(i):
        return pl.ds(pl.multiple_of(i * 128, 128), 128)

    mine = half(layer)
    cols = pl.ds(pl.multiple_of(p * PAIR, 128), PAIR)
    real = pl.ds(0, ROWS)

    def has_tile(yy, xx):
        return jnp.logical_not(jnp.logical_and(yy % 2 == 1, xx == 3))

    owns = has_tile(y, x)

    def remote(src, dst, send, recv, dev):
        return pltpu.make_async_remote_copy(
            src_ref=src, dst_ref=dst, send_sem=send, recv_sem=recv, device_id=dev, device_id_type=MESH
        )

    local = []
    for c in range(CHUNKS):
        local.append(pltpu.make_async_copy(taps.at[pl.ds(TILES * c, 4), :, cols], x_t.at[c, 0, 0, 0], loc.at[2 * c]))
        local.append(
            pltpu.make_async_copy(
                taps.at[pl.ds(TILES * c + 4, 3), :, cols], x_t.at[c, 0, 0, 1, pl.ds(0, 3)], loc.at[2 * c + 1]
            )
        )
    ids_cp = pltpu.make_async_copy(ids_in, ids, loc.at[2 * CHUNKS])
    ids_cp.start()
    local.append(pltpu.make_async_copy(eb.at[:, mine], bias, loc.at[2 * CHUNKS + 1]))
    local.append(pltpu.make_async_copy(db.at[:, cols], dbias, loc.at[2 * CHUNKS + 2]))
    local.append(pltpu.make_async_copy(we, w_e.at[r], loc.at[2 * CHUNKS + 3]))
    local.append(pltpu.make_async_copy(wd, w_d.at[r], loc.at[2 * CHUNKS + 4]))
    for cp in local:
        cp.start()

    for c in range(CHUNKS):
        for q in range(4):
            x_t[c, q // 2, q % 2, 1, 3] = jnp.zeros((16, PAIR), BF16)
            res[c, q // 2, q % 2, 1, 3] = jnp.zeros((16, PAIR), BF16)
    barrier = pltpu.get_barrier_semaphore()
    partners = [far, other_core, twin] + [zpeer(k) for k in (1, 2, 3)]
    partners += [chip((y + k) % 4, x) for k in (1, 2, 3)] + [chip(y, (x + k) % 4) for k in (1, 2, 3)]
    for dev in partners:
        pl.semaphore_signal(barrier, inc=1, device_id=dev, device_id_type=MESH)
    for c in range(CHUNKS):
        for q in range(4):
            for i in range(2):
                feat[c, i, q, ROWS:] = jnp.zeros((16, 128), BF16)
                pg[c, i, q, ROWS:] = jnp.zeros((16, 128), BF16)
            keep[c, q, ROWS:] = jnp.zeros((16, 128), F32)
    ids_cp.wait()
    keep_row = (ids[...] != BEGIN_TOKEN).astype(F32)
    mask[0] = jnp.broadcast_to(keep_row, mask.shape[1:]).astype(BF16)
    for cp in local:
        cp.wait()
    pl.semaphore_wait(barrier, len(partners))

    sends, pending, step = [], {}, {}

    def under(when, action):
        if when is None:
            action()
        else:
            pl.when(when)(action)

    def go(cp, when=None, arrives=None):
        under(when, cp.start)
        sends.append((cp, when))
        pending[len(sends)] = (cp, arrives)
        return len(sends)

    def got(*entries):
        for entry in entries:
            cp, arrives = pending.pop(entry)
            under(arrives, cp.wait_recv)

    def finish():
        got(*list(pending))
        for cp, when in sends:
            under(when, cp.wait_send)

    def both(a, b):
        return b if a is None else jnp.logical_and(a, b)

    def spread_first(buf, c, send, recv, rows=None):
        out = []
        for k in (1, 2, 3):
            xx, yy = (x + k) % 4, (y + k) % 4
            for u, dev, source in (
                (0, chip(y, xx), has_tile(y, (x + 4 - k) % 4)),
                (1, chip(yy, x), has_tile((y + 4 - k) % 4, x)),
            ):
                part = buf.at[c, y // 2, u, y % 2, x]
                lead = rows if u == 0 else None
                out.append(
                    go(remote(part, part, send.at[0, c, u, k - 1], recv.at[0, c, u, k - 1], dev),
                       both(lead, owns), both(lead, source))
                )
        return out

    def spread_second(buf, c, send, recv, rows=None):
        out = []
        for k in (1, 2, 3):
            xx, yy = (x + k) % 4, (y + k) % 4
            part = buf.at[c, y // 2, 0, y % 2]
            out.append(
                go(remote(part, part, send.at[1, c, 0, k - 1], recv.at[1, c, 0, k - 1], chip(yy, x)),
                   rows, None if rows is None else (y + 4 - k) % 4 >= 2)
            )
            part = buf.at[c, pl.ds(0, 2), 1, pl.ds(0, 2), x]
            out.append(go(remote(part, part, send.at[1, c, 1, k - 1], recv.at[1, c, 1, k - 1], chip(y, xx))))
        return out

    low = y >= 2
    tile = 4 * (y % 2) + x
    for c in range(CHUNKS):
        entries = []
        for k in (1, 2, 3):
            q = 4 - k
            there = pl.ds(pl.multiple_of(((p + k) % 4) * PAIR, 128), PAIR)
            when = both(low if q >= 2 else jnp.logical_not(low), owns)
            src = taps.at[lax.min(TILES * c + tile, taps.shape[0] - 1), :, there]
            dst = x_t.at[c, q // 2, q % 2, y % 2, x]
            entries.append(go(remote(src, dst, xz_s.at[c, k - 1], xz_r.at[c, q - 1], zpeer(k)), when, when))
        step["xz", c] = entries
    mask_cp = [go(remote(mask.at[0], mask.at[4 - k], mk_s.at[k - 1], mk_r.at[3 - k], zpeer(k))) for k in (1, 2, 3)]

    def taps_first(c):
        got(*step["xz", c])
        step["xa", c] = spread_first(x_t, c, xy_s, xy_r, low)
        if c == 0:
            step["we"] = go(remote(we, w_e.at[r], one_s.at[0], one_r.at[0], twin))
        if c == CHUNKS - 1:
            step["wd"] = go(remote(wd, w_d.at[r], one_s.at[1], one_r.at[1], twin))

    def taps_second(c):
        got(*step["xa", c])
        step["xb", c] = spread_second(x_t, c, xy_s, xy_r, low)

    def norms_first(c):
        w_sq = jnp.square(w_d[...].astype(F32)).reshape(PAIR, 256)
        nsq[0] = jnp.broadcast_to(jnp.sum(w_sq, axis=0, keepdims=True), (8, 256))
        step["ns"] = [
            go(remote(nsq.at[0], nsq.at[4 - k], ns_s.at[k - 1], ns_r.at[3 - k], zpeer(k))) for k in (1, 2, 3)
        ]
        got(*mask_cp)
        unit = jnp.full((16, 128), 1.0 / 16.0, BF16)
        for q in range(4):
            column = lax.dot_general(mask[q], unit, (((0,), (0,)), ((), ())), preferred_element_type=F32)
            for c in range(CHUNKS):
                keep[c, q, :ROWS] = column[c * ROWS:(c + 1) * ROWS]

    def norms_second(c):
        got(*step["ns"])
        cnorm[...] = jnp.sqrt(nsq[0] + nsq[1] + nsq[2] + nsq[3] + 1e-06)
        step["cn"] = go(remote(cnorm, cnorm_o, one_s.at[2], one_r.at[2], other_core))

    def z_group(sem, src, dst, c):
        return [
            go(remote(src(k), dst(4 - k), zg_s.at[sem, c, k - 1], zg_r.at[sem, c, 3 - k], zpeer(k)))
            for k in (1, 2, 3)
        ]

    def cross(c, sem, part, own_ref, out_ref, got_ref):
        part = part.reshape(4, PADDED, 256)[:, :ROWS]
        is_low = layer == 0
        own_ref[c] = jnp.where(is_low, part[:, :, :128], part[:, :, 128:])
        out_ref[c] = jnp.where(is_low, part[:, :, 128:], part[:, :, :128]).astype(BF16)
        return go(remote(out_ref.at[c], got_ref.at[c], co_s.at[sem, c], co_r.at[sem, c], other_core))

    def cross_half(c, sem, full):
        block = full.at[c, layer, :, real]
        return go(remote(block, block, co_s.at[sem, c], co_r.at[sem, c], other_core))

    def rows_of(ref, c):
        return ref[c].reshape(4 * PADDED, ref.shape[-1])

    def wide(ref, c):
        return jnp.concatenate([ref[c, i].reshape(4 * PADDED, 128) for i in range(2)], axis=1)

    def pre_dot(c):
        got(*step["xb", c])
        if c == 0:
            got(step["we"])
        part = jnp.dot(rows_of(x_t, c), w_e[...].reshape(PAIR, 256), preferred_element_type=F32)
        step["pc", c] = cross(c, 0, part, pre_f, pre_o, pre_x)

    def pre_sum(c):
        got(step["pc", c])
        for q in (1, 2, 3):
            pre_s[c, q - 1] = (pre_f[c, q] + pre_x[c, q].astype(F32)).astype(BF16)
        step["pz", c] = z_group(0, lambda k: pre_s.at[c, k - 1], lambda q: pre_r.at[c, q - 1], c)
        pre_own[c] = pre_f[c, 0] + pre_x[c, 0].astype(F32)

    def pre_act(c):
        got(*step["pz", c])
        preact = pre_own[c] + bias[...]
        for q in range(3):
            preact = preact + pre_r[c, q].astype(F32)
        pre_own[c] = preact
        feat[c, layer, 0, :ROWS] = smooth_relu(preact).astype(BF16)
        step["fz", c] = z_group(1, lambda k: feat.at[c, layer, 0, real], lambda q: feat.at[c, layer, q, real], c)

    def feat_cross(c):
        got(*step["fz", c])
        step["fc", c] = cross_half(c, 1, feat)

    def reb_dot(c):
        got(step["fc", c])
        if c == 0:
            got(step["wd"])
        part = lax.dot_general(
            wide(feat, c), w_d[...].reshape(PAIR, 256), (((1,), (1,)), ((), ())), preferred_element_type=F32
        )
        reb[c] = part.astype(BF16).reshape(2, 2, 2, 4, 16, PAIR)
        step["ra", c] = []
        for k in (1, 2, 3):
            xx, yy = (x + k) % 4, (y + k) % 4
            step["ra", c].append(go(remote(
                reb.at[c, pl.ds(0, 2), 0, pl.ds(0, 2), xx], row_r.at[c, k - 1],
                rr_s.at[0, c, 0, k - 1], rr_r.at[0, c, 0, k - 1], chip(y, xx))))
            step["ra", c].append(go(remote(
                reb.at[c, yy // 2, 1, yy % 2], col_r.at[c, k - 1],
                rr_s.at[0, c, 1, k - 1], rr_r.at[0, c, 1, k - 1], chip(yy, x))))

    def reb_mid(c):
        got(*step["ra", c])
        total = reb[c, :, 0, :, x].astype(F32)
        for k in range(3):
            total = total + row_r[c, k].astype(F32)
        row_s[c] = total.astype(BF16)
        own_s[c, 0] = row_s[c, y // 2, y % 2]
        total = reb[c, y // 2, 1, y % 2].astype(F32)
        for k in range(3):
            total = total + col_r[c, k].astype(F32)
        col_s[c] = total.astype(BF16)
        own_s[c, 1] = col_s[c, x]
        step["rb", c] = []
        for k in (1, 2, 3):
            xx, yy = (x + k) % 4, (y + k) % 4
            step["rb", c].append(go(remote(
                row_s.at[c, yy // 2, yy % 2], end_r.at[c, k - 1, 0],
                rr_s.at[1, c, 0, k - 1], rr_r.at[1, c, 0, k - 1], chip(yy, x)), has_tile(yy, x), owns))
            step["rb", c].append(go(remote(
                col_s.at[c, xx], end_r.at[c, k - 1, 1],
                rr_s.at[1, c, 1, k - 1], rr_r.at[1, c, 1, k - 1], chip(y, xx)), has_tile(y, xx), owns))

    def reb_sum(c):
        got(*step["rb", c])

        @pl.when(owns)
        def _():
            total = own_s[c].astype(F32)
            for k in range(3):
                total = total + end_r[c, k].astype(F32)
            zs[c] = total
            zb[c] = total.astype(BF16)

        step["zh", c] = go(remote(zb.at[c], zr.at[c], zh_s.at[c], zh_r.at[c], far), owns, owns)

    def residue(c):
        got(step["zh", c])

        @pl.when(owns)
        def _():
            rebuilt = zs[c] + zr[c].astype(F32) + dbias[...].reshape(1, 1, PAIR)
            diff = rebuilt - x_t[c, y // 2, :, y % 2, x].astype(F32)
            spot = pl.ds(pl.multiple_of(16 * tile, 16), 16)
            weight = loss_scale * keep[c, pl.ds(2 * (y // 2), 2), spot][:, :, :1]
            res[c, y // 2, :, y % 2, x] = (weight * diff).astype(BF16)

        step["sa", c] = spread_first(res, c, rs_s, rs_r)

    def residue_second(c):
        got(*step["sa", c])
        step["sb", c] = spread_second(res, c, rs_s, rs_r)

    def grad_dot(c):
        got(*step["sb", c])
        part = jnp.dot(rows_of(res, c), w_d[...].reshape(PAIR, 256), preferred_element_type=F32)
        step["gc", c] = cross(c, 2, part, g_f, g_o, g_x)

    def grad_sum(c):
        got(step["gc", c])
        for q in (1, 2, 3):
            g_s[c, q - 1] = (g_f[c, q] + g_x[c, q].astype(F32)).astype(BF16)
        step["gz", c] = z_group(2, lambda k: g_s.at[c, k - 1], lambda q: g_r.at[c, q - 1], c)
        g_own[c] = g_f[c, 0] + g_x[c, 0].astype(F32)

    def grad_pre(c):
        if c == 0:
            got(step["cn"])
        got(*step["gz", c])
        norm_total = cnorm[0:1, mine] + cnorm_o[0:1, mine]
        grads = g_own[c] + loss_scale * SPARSITY * keep[c, 0, :ROWS] * norm_total
        for q in range(3):
            grads = grads + g_r[c, q].astype(F32)
        pg[c, layer, 0, :ROWS] = (grads * relu_slope(pre_own[c])).astype(BF16)
        step["qz", c] = z_group(3, lambda k: pg.at[c, layer, 0, real], lambda q: pg.at[c, layer, q, real], c)

    def grad_cross(c):
        got(*step["qz", c])
        step["qc", c] = cross_half(c, 3, pg)

    def dec_grad(c):
        f = wide(feat, c)
        active = jnp.sum(rows_of(keep, c)[:, :1] * f.astype(F32), axis=0, keepdims=True)
        penalty = loss_scale * SPARSITY * active / cnorm[0:1, :]
        total = w_d[...].reshape(PAIR, 256).astype(F32) * penalty + lax.dot_general(
            rows_of(res, c), f, (((0,), (0,)), ((), ())), preferred_element_type=F32
        )
        total = total.reshape(2, PAIR // 2, 256)
        dwd[...] = total if c == 0 else dwd[...] + total
        if c == CHUNKS - 1:
            dwd_s[...] = dwd[1 - r].astype(BF16)
            step["dwd"] = go(remote(dwd_s, dwd_r, one_s.at[3], one_r.at[3], twin))

    def enc_grad(c):
        got(step["qc", c])
        total = lax.dot_general(
            rows_of(x_t, c), wide(pg, c), (((0,), (0,)), ((), ())), preferred_element_type=F32
        ).reshape(2, PAIR // 2, 256)
        dwe[...] = total if c == 0 else dwe[...] + total
        if c == CHUNKS - 1:
            dwe_s[...] = dwe[1 - r].astype(BF16)
            step["dwe"] = go(remote(dwe_s, dwe_r, one_s.at[4], one_r.at[4], twin))

    stages = {
        "taps_first": taps_first,
        "taps_second": taps_second,
        "pre_dot": pre_dot,
        "pre_sum": pre_sum,
        "pre_act": pre_act,
        "feat_cross": feat_cross,
        "reb_dot": reb_dot,
        "reb_mid": reb_mid,
        "reb_sum": reb_sum,
        "residue": residue,
        "residue_second": residue_second,
        "grad_dot": grad_dot,
        "grad_sum": grad_sum,
        "grad_pre": grad_pre,
        "grad_cross": grad_cross,
        "enc_grad": enc_grad,
        "dec_grad": dec_grad,
        "norms_first": norms_first,
        "norms_second": norms_second,
    }
    for stage, c in ORDER:
        stages[stage](c)
    got(step["dwd"])
    dec_out[...] = (dwd[r] + dwd_r[...].astype(F32)).astype(BF16)
    got(step["dwe"])
    enc_out[...] = (dwe[r] + dwe_r[...].astype(F32)).astype(BF16)
    finish()


def local(taps, token_ids, enc_weight, enc_bias, dec_weight, dec_bias):
    tokens_dev = taps.shape[1]
    loss_scale = 1.0 / math.sqrt(tokens_dev * lax.axis_size("token"))
    c = CHUNKS
    dma = pltpu.SemaphoreType.DMA
    vmem = pltpu.VMEM
    tiles = (c, 2, 2, 2, 4, 16, PAIR)
    scratch = [
        vmem((1, tokens_dev), jnp.int32), vmem((1, 128), F32), vmem((1, PAIR), F32),
        vmem(tiles, BF16),
        vmem((2, 448, 256), BF16), vmem((2, 448, 256), BF16),
        vmem((4, 16, 224), BF16), vmem((c, 4, PADDED, 128), F32),
        vmem((4, 8, 256), F32), vmem((8, 256), F32), vmem((8, 256), F32),
        vmem((c, 4, ROWS, 128), F32), vmem((c, 4, ROWS, 128), BF16), vmem((c, 4, ROWS, 128), BF16),
        vmem((c, 3, ROWS, 128), BF16), vmem((c, 3, ROWS, 128), BF16), vmem((c, ROWS, 128), F32),
        vmem((c, 2, 4, PADDED, 128), BF16),
        vmem(tiles, BF16),
        vmem((c, 3, 2, 2, 16, PAIR), BF16), vmem((c, 3, 4, 16, PAIR), BF16),
        vmem((c, 2, 2, 16, PAIR), BF16), vmem((c, 4, 16, PAIR), BF16),
        vmem((c, 2, 16, PAIR), BF16), vmem((c, 3, 2, 16, PAIR), BF16),
        vmem((c, 2, 16, PAIR), F32), vmem((c, 2, 16, PAIR), BF16), vmem((c, 2, 16, PAIR), BF16),
        vmem(tiles, BF16),
        vmem((c, 4, ROWS, 128), F32), vmem((c, 4, ROWS, 128), BF16), vmem((c, 4, ROWS, 128), BF16),
        vmem((c, 3, ROWS, 128), BF16), vmem((c, 3, ROWS, 128), BF16), vmem((c, ROWS, 128), F32),
        vmem((c, 2, 4, PADDED, 128), BF16),
        vmem((2, 448, 256), F32), vmem((448, 256), BF16), vmem((448, 256), BF16),
        vmem((2, 448, 256), F32), vmem((448, 256), BF16), vmem((448, 256), BF16),
        dma((2 * c + 5,)),
        dma((c, 3)), dma((c, 3)), dma((2, c, 2, 3)), dma((2, c, 2, 3)),
        dma((3,)), dma((3,)), dma((3,)), dma((3,)),
        dma((5,)), dma((5,)),
        dma((4, c)), dma((4, c)), dma((4, c, 3)), dma((4, c, 3)),
        dma((2, c, 2, 3)), dma((2, c, 2, 3)), dma((c,)), dma((c,)), dma((2, c, 2, 3)), dma((2, c, 2, 3)),
    ]
    any_spec = pl.BlockSpec(memory_space=pl.ANY)
    vmem_spec = pl.BlockSpec(memory_space=pltpu.VMEM)
    enc_grad, dec_grad = pl.pallas_call(
        functools.partial(kernel, loss_scale),
        out_shape=(jax.ShapeDtypeStruct((448, 256), BF16), jax.ShapeDtypeStruct((448, 256), BF16)),
        in_specs=[any_spec] * 6,
        out_specs=(vmem_spec, vmem_spec),
        scratch_shapes=scratch,
        compiler_params=pltpu.CompilerParams(
            collective_id=0, has_side_effects=True, vmem_limit_bytes=60 * 1024 * 1024
        ),
        name="crosscoder",
    )(taps.reshape(tokens_dev // 16, 16, taps.shape[2]), token_ids[None, :], enc_weight[0], enc_bias[None, :], dec_weight[0], dec_bias)
    return enc_grad[None], dec_grad[None]


def solution(mesh):
    placed = (
        P("layer", "token", None),
        P("token"),
        P("layer", "token", "latent"),
        P("latent"),
        P("layer", "token", "latent"),
        P("layer", None),
    )
    return jax.shard_map(
        local,
        mesh=mesh,
        in_specs=placed,
        out_specs=(P("layer", "token", "latent"), P("layer", "token", "latent")),
        check_vma=False,
    )
```
